32 devices in a mesh: wave: 2 (over x), region: 16 (over z, y, core).
Axes of the slice: x: 2, y: 2, z: 4, core: 2. Of those that a mesh axis runs over, the one named last changes fastest.
Arguments:
- object_field: float32 [2, 8192, 1024], P(None, 'region'), may hold values from -5 to 5
- probes: float32 [2, 2, 256, 256], P('wave'), may hold values from -5 to 5
- patterns: bfloat16 [2, 256, 256, 256], P('wave', 'region'), may hold values from 0 to 2
- offsets: int32 [256, 2], P('region'), may hold values from 0 to 768, as said below
- counts: int32 [16], P('region'), may hold values from 1 to 16, as said below
Outputs:
- object_grad: float32 [2, 8192, 1024], P(None, 'region', 'wave')
- probe_grad: float32 [2, 2, 256, 256], P('wave')
The draws below stay inside these ranges and needn't reach their ends.
Inputs may be any that keep to these rules, and one draw needn't show every extreme that they name: Offsets are whole cells: row offsets below 512, column offsets at most 768. `counts`: some tile uses all slots and some tile uses one.
All inputs are finite; a program needn't handle non-finite values.
Results may differ from the reference program's by a relative error of at most 0.0052.
Values sent between devices are 32-bit elements; how exact they have to be, the bound alone decides.
A program may use at most 128 MiB of HBM per device.

```python
import math
import jax
import jax.numpy as jnp
from jax import lax

PATCH = 256
TILE = 512
WIDTH = 1024
POS = 16
WAVES = 2
ROWS = 8192
POSITIONS = 256


def draw_offsets(key, part):
    first_key, second_key = jax.random.split(jax.random.fold_in(key, 11))
    row_vals = jax.random.randint(first_key, (POSITIONS,), 0, TILE, dtype=jnp.int32)
    col_vals = jax.random.randint(second_key, (POSITIONS,), 0, WIDTH - PATCH + 1, dtype=jnp.int32)
    row_vals = row_vals.at[0].set(TILE - 1).at[1].set(0)
    col_vals = col_vals.at[2].set(WIDTH - PATCH).at[3].set(0)
    return jnp.stack([row_vals, col_vals], axis=1).astype(jnp.int32)


def draw_counts(key, part):
    first_key, second_key = jax.random.split(jax.random.fold_in(key, 23))
    tiles = POSITIONS // POS
    base_vals = jax.random.randint(first_key, (tiles,), 1, POS + 1, dtype=jnp.int32)
    order = jax.random.permutation(second_key, tiles)
    base_vals = base_vals.at[order[0]].set(POS).at[order[1]].set(1)
    return base_vals.astype(jnp.int32)


def steps_of(rng, shape, cuts, least, largest):
    level = 1.0
    for dim, parts in cuts:
        draws = jax.random.uniform(jax.random.fold_in(jax.random.fold_in(rng, 6), dim), (parts,), jnp.float32, least / len(cuts), largest / len(cuts))
        level = level * jnp.repeat(jnp.exp(draws), shape[dim] // parts).reshape((-1,) + (1,) * (len(shape) - 1 - dim))
    return level


def scatter_about(stream_key, dims, spread, reach, pieces=(), kind=jnp.bfloat16):
    values = jax.random.normal(stream_key, dims, jnp.float32) * spread
    if len(pieces) > 0:
        values = steps_of(stream_key, dims, pieces, -0.22, 0.18) * values
    return jnp.clip(values, min=-reach, max=reach).astype(kind)


def setup_inputs(seed: int = 0) -> dict:
    streams_of = jax.random.split(jax.random.key(seed), 6)
    object_field = scatter_about(streams_of[0], (2, ROWS, WIDTH), 0.7, 5.0, ((1, 16),), jnp.float32)
    probes = scatter_about(streams_of[1], (WAVES, 2, PATCH, PATCH), 0.7, 5.0, ((0, 2),), jnp.float32)
    patterns = jnp.clip(2.0 * jax.random.uniform(streams_of[2], (WAVES, POSITIONS, PATCH, PATCH), jnp.float32) ** steps_of(streams_of[2], (WAVES, POSITIONS, PATCH, PATCH), ((0, 2), (1, 16)), -0.2, 0.2), 0.0, 2.0).astype(jnp.bfloat16)
    offsets = draw_offsets(jax.random.fold_in(streams_of[5], 71), 0)
    counts = draw_counts(jax.random.fold_in(streams_of[5], 71), 0)
    return dict(object_field=object_field, probes=probes, patterns=patterns, offsets=offsets, counts=counts)


def make_tables():
    index = jnp.arange(PATCH, dtype=jnp.int32)
    phase_int = index[:, None] * index[None, :] % PATCH
    phase = phase_int.astype(jnp.float32) * (2.0 * math.pi / PATCH)
    scale = 1.0 / math.sqrt(PATCH)
    cos_table = (jnp.cos(phase) * scale).astype(jnp.bfloat16).astype(jnp.float32)
    sin_table = (jnp.sin(phase) * scale).astype(jnp.bfloat16).astype(jnp.float32)
    return (cos_table, sin_table)

def to_grid(value):
    return lax.optimization_barrier(value.astype(jnp.bfloat16)).astype(jnp.float32)

def apply_left(table, field_part):
    return jnp.einsum('kn,wnm->wkm', table, field_part)

def apply_right(field_part, table):
    return jnp.einsum('wkn,nm->wkm', field_part, table)

def reference(object_field, probes, patterns, offsets, counts):
    cos_table, sin_table = make_tables()
    padded = jnp.concatenate([object_field, jnp.zeros((2, PATCH, WIDTH), jnp.float32)], axis=1)
    probe_re = probes[:, 0]
    probe_im = probes[:, 1]

    def advance(state_pair, slot):
        grad_ext, probe_acc = state_pair
        tile_index = slot // POS
        slot_index = slot % POS
        row_at = (tile_index * TILE + offsets[slot, 0]).astype(jnp.int32)
        col_at = offsets[slot, 1].astype(jnp.int32)
        zero_at = jnp.zeros((), jnp.int32)
        patch_cut = lax.dynamic_slice(padded, (zero_at, row_at, col_at), (2, PATCH, PATCH))
        wave_re = to_grid(probe_re * patch_cut[0] - probe_im * patch_cut[1])
        wave_im = to_grid(probe_re * patch_cut[1] + probe_im * patch_cut[0])
        half_re = to_grid(apply_left(cos_table, wave_re) + apply_left(sin_table, wave_im))
        half_im = to_grid(apply_left(cos_table, wave_im) - apply_left(sin_table, wave_re))
        far_re = apply_right(half_re, cos_table) + apply_right(half_im, sin_table)
        far_im = apply_right(half_im, cos_table) - apply_right(half_re, sin_table)
        measured = lax.dynamic_index_in_dim(patterns, slot, 1, keepdims=False).astype(jnp.float32)
        excess = far_re * far_re + far_im * far_im - measured
        back_re = to_grid(excess * far_re)
        back_im = to_grid(excess * far_im)
        inner_re = to_grid(apply_left(cos_table, back_re) - apply_left(sin_table, back_im))
        inner_im = to_grid(apply_left(cos_table, back_im) + apply_left(sin_table, back_re))
        chi_re = apply_right(inner_re, cos_table) - apply_right(inner_im, sin_table)
        chi_im = apply_right(inner_im, cos_table) + apply_right(inner_re, sin_table)
        in_use = (slot_index < counts[tile_index]).astype(jnp.float32)
        obj_re = lax.optimization_barrier(jnp.sum(probe_re * chi_re + probe_im * chi_im, axis=0)) * in_use
        obj_im = lax.optimization_barrier(jnp.sum(probe_re * chi_im - probe_im * chi_re, axis=0)) * in_use
        current = lax.dynamic_slice(grad_ext, (zero_at, row_at, col_at), (2, PATCH, PATCH))
        grad_ext = lax.dynamic_update_slice(grad_ext, current + jnp.stack([obj_re, obj_im]), (zero_at, row_at, col_at))
        prb_re = (patch_cut[0] * chi_re + patch_cut[1] * chi_im) * in_use
        prb_im = (patch_cut[0] * chi_im - patch_cut[1] * chi_re) * in_use
        probe_acc = probe_acc + jnp.stack([prb_re, prb_im], axis=1)
        return ((grad_ext, probe_acc), None)
    start_state = (jnp.zeros((2, ROWS + PATCH, WIDTH), jnp.float32), jnp.zeros((WAVES, 2, PATCH, PATCH), jnp.float32))
    (grad_ext, probe_acc), _ = lax.scan(advance, start_state, jnp.arange(POSITIONS, dtype=jnp.int32))
    return (grad_ext[:, :ROWS], probe_acc)
```

```python
import functools
import math

import jax
import jax.numpy as jnp
import numpy as np
from jax import lax
from jax.experimental import pallas as pl
from jax.experimental.pallas import tpu as pltpu
from jax.sharding import PartitionSpec as P

STRIP = 32
LANES = 128
UNROLL = 2
VMEM_LIMIT = 56 * 1024 * 1024


def from_behind(block, axis, distance):
    devices = range(lax.axis_size(axis))
    route = [(i - distance, i) for i in devices if i - distance in devices]
    return lax.ppermute(block, axis, route)


def make_tables(side):
    index = np.arange(side)
    phase = (index[:, None] * index[None, :] % side) * (2.0 * math.pi / side)
    cos = (np.cos(phase) / math.sqrt(side)).astype(np.float32)
    sin = (np.sin(phase) / math.sqrt(side)).astype(np.float32)
    forward = np.block([[cos, sin], [-sin, cos]])
    inverse = np.block([[cos, -sin], [sin, cos]])
    return jnp.asarray(forward, jnp.bfloat16), jnp.asarray(inverse, jnp.bfloat16)


def patch_kernel(second, side, slots, width, *refs):
    offs, count, field, *refs = refs
    if second:
        rim, grad_in, prb_in, *refs = refs
    probe, patterns, forward, inverse = refs[:4]
    grad, prb = refs[4:6]
    ext, pats, order, sems = refs[6:10]
    patch = refs[10 : 10 + UNROLL]
    wave = refs[10 + UNROLL : 10 + 2 * UNROLL]
    half = refs[10 + 2 * UNROLL : 10 + 3 * UNROLL]
    far = refs[10 + 3 * UNROLL : 10 + 4 * UNROLL]
    base = side if second else 0

    copies = [pltpu.make_async_copy(patterns.at[0], pats, sems.at[0])]
    if second:
        copies += [
            pltpu.make_async_copy(
                grad_in.at[:, :, pl.ds(side, side)], grad.at[:, :, pl.ds(0, side)], sems.at[1]
            ),
        ]
    for k in range(width // LANES):
        cols = pl.ds(k * LANES, LANES)
        if second:
            copies += [
                pltpu.make_async_copy(
                    field.at[:, pl.ds(side, side), cols], ext.at[k, :, pl.ds(0, side)], sems.at[2 + 2 * k]
                ),
                pltpu.make_async_copy(
                    rim.at[:, :, cols], ext.at[k, :, pl.ds(side, side)], sems.at[3 + 2 * k]
                ),
            ]
        else:
            copies += [pltpu.make_async_copy(field.at[:, :, cols], ext.at[k], sems.at[2 + 2 * k])]
    for copy in copies:
        copy.start()

    if second:
        grad[:, :, side:, :] = jnp.zeros((width // LANES, 2, side, LANES), jnp.float32)
        prb[...] = prb_in[...]
    else:
        grad[...] = jnp.zeros_like(grad)
        prb[...] = jnp.zeros_like(prb)

    def gather(slot, found):
        row = offs[slot, 0]
        inside = (row >= side) if second else (row < side)
        take = inside & (slot < count[0])

        @pl.when(take)
        def _():
            order[found] = slot

        return found + take.astype(jnp.int32)

    for lane in range(UNROLL):
        order[slots + lane] = 0
    total = lax.fori_loop(0, slots, gather, jnp.int32(0))
    for lane in range(UNROLL):
        order[total + lane] = 0
    for copy in copies:
        copy.wait()

    chunks = side // LANES
    lane_id = lax.broadcasted_iota(jnp.int32, (STRIP, LANES), 1)

    def place(position):
        slot = order[position]
        row = jnp.clip(offs[slot, 0] - base, 0, side - 1)
        col = offs[slot, 1]
        start = jnp.minimum(col // LANES, width // LANES - chunks - 1)
        return slot, row, start, col - start * LANES

    def body(step, carry):
        placed = [place(step * UNROLL + u) for u in range(UNROLL)]
        for u in range(UNROLL):
            slot, row, start, shift = placed[u]
            back_shift = lax.rem(LANES - shift, LANES)
            for s in range(side // STRIP):
                at = slice(s * STRIP, (s + 1) * STRIP)
                parts = []
                for plane in range(2):
                    rolled = [
                        pltpu.roll(
                            ext[start + k, plane, pl.ds(row + s * STRIP, STRIP), :],
                            back_shift,
                            1,
                        )
                        for k in range(chunks + 1)
                    ]
                    parts.append(
                        [
                            jnp.where(lane_id < LANES - shift, rolled[k], rolled[k + 1])
                            for k in range(chunks)
                        ]
                    )
                for k in range(chunks):
                    cols = slice(k * LANES, (k + 1) * LANES)
                    re, im = parts[0][k], parts[1][k]
                    p_re, p_im = probe[0, 0, at, cols], probe[0, 1, at, cols]
                    patch[u][0, at, cols] = re
                    patch[u][1, at, cols] = im
                    wave[u][at, cols] = (p_re * re - p_im * im).astype(jnp.bfloat16)
                    wave[u][side + s * STRIP : side + (s + 1) * STRIP, cols] = (
                        p_re * im + p_im * re
                    ).astype(jnp.bfloat16)
        for u in range(UNROLL):
            product = jnp.dot(forward[...], wave[u][...], preferred_element_type=jnp.float32)
            half[u][:, :side] = product[:side].astype(jnp.bfloat16)
            half[u][:, side:] = product[side:].astype(jnp.bfloat16)
        for u in range(UNROLL):
            far[u][...] = jnp.dot(half[u][...], inverse[...], preferred_element_type=jnp.float32)
        for u in range(UNROLL):
            slot = placed[u][0]
            for s in range(side // STRIP):
                at = slice(s * STRIP, (s + 1) * STRIP)
                f_re, f_im = far[u][at, :side], far[u][at, side:]
                seen = pats[slot, at, :].astype(jnp.float32)
                excess = f_re * f_re + f_im * f_im - seen
                wave[u][at, :] = (excess * f_re).astype(jnp.bfloat16)
                wave[u][side + s * STRIP : side + (s + 1) * STRIP, :] = (excess * f_im).astype(
                    jnp.bfloat16
                )
        for u in range(UNROLL):
            product = jnp.dot(inverse[...], wave[u][...], preferred_element_type=jnp.float32)
            half[u][:, :side] = product[:side].astype(jnp.bfloat16)
            half[u][:, side:] = product[side:].astype(jnp.bfloat16)
        for u in range(UNROLL):
            far[u][...] = jnp.dot(half[u][...], forward[...], preferred_element_type=jnp.float32)
        for u in range(UNROLL):
            slot, row, start, shift = placed[u]
            valid = (step * UNROLL + u < total).astype(jnp.float32)
            for s in range(side // STRIP):
                at = slice(s * STRIP, (s + 1) * STRIP)
                terms = [[], []]
                for k in range(chunks):
                    cols = slice(k * LANES, (k + 1) * LANES)
                    c_re = far[u][at, cols] * valid
                    c_im = far[u][at, side + k * LANES : side + (k + 1) * LANES] * valid
                    re, im = patch[u][0, at, cols], patch[u][1, at, cols]
                    prb[0, at, cols] += re * c_re + im * c_im
                    prb[1, at, cols] += re * c_im - im * c_re
                    p_re, p_im = probe[0, 0, at, cols], probe[0, 1, at, cols]
                    terms[0].append(p_re * c_re + p_im * c_im)
                    terms[1].append(p_re * c_im - p_im * c_re)
                for plane in range(2):
                    rolled = [pltpu.roll(t, lax.rem(shift, LANES), 1) for t in terms[plane]]
                    rolled = [jnp.zeros_like(rolled[0])] + rolled + [jnp.zeros_like(rolled[0])]
                    for k in range(chunks + 1):
                        where = (start + k, plane, pl.ds(row + s * STRIP, STRIP))
                        grad[where] += jnp.where(lane_id >= shift, rolled[k + 1], rolled[k])
        return carry

    lax.fori_loop(0, (total + UNROLL - 1) // UNROLL, body, 0)


def patch_call(second, offsets, counts, field, extra, probes, patterns, tables):
    side = probes.shape[-1]
    slots = offsets.shape[0]
    width = field.shape[2]
    smem = pl.BlockSpec(memory_space=pltpu.SMEM)
    vmem = pl.BlockSpec(memory_space=pltpu.VMEM)
    hbm = pl.BlockSpec(memory_space=pl.ANY)
    specs = [smem, smem, hbm] + ([hbm, hbm, vmem] if second else []) + [vmem, hbm, vmem, vmem]
    scratch = [
        pltpu.VMEM((width // LANES, 2, 2 * side, LANES), jnp.float32),
        pltpu.VMEM((slots, side, side), jnp.bfloat16),
        pltpu.SMEM((slots + UNROLL,), jnp.int32),
        pltpu.SemaphoreType.DMA((2 + 2 * (width // LANES),)),
    ]
    scratch += [pltpu.VMEM((2, side, side), jnp.float32)] * UNROLL
    scratch += [pltpu.VMEM((2 * side, side), jnp.bfloat16)] * UNROLL
    scratch += [pltpu.VMEM((side, 2 * side), jnp.bfloat16)] * UNROLL
    scratch += [pltpu.VMEM((side, 2 * side), jnp.float32)] * UNROLL
    return pl.pallas_call(
        functools.partial(patch_kernel, second, side, slots, width),
        out_shape=(
            jax.ShapeDtypeStruct((width // LANES, 2, 2 * side, LANES), jnp.float32),
            jax.ShapeDtypeStruct((2, side, side), jnp.float32),
        ),
        in_specs=specs,
        out_specs=(vmem, vmem),
        scratch_shapes=scratch,
        compiler_params=pltpu.CompilerParams(vmem_limit_bytes=VMEM_LIMIT),
        cost_estimate=pl.CostEstimate(
            flops=slots * 16 * side**3, bytes_accessed=20 * 1024 * 1024, transcendentals=0
        ),
        name="second_half" if second else "first_half",
    )(offsets, counts, field, *extra, probes, patterns, *tables)


def wave_sum(block):
    waves = lax.axis_size("wave")
    share = block.shape[0] // waves
    if waves == 2:
        me = lax.axis_index("wave")
        give = lax.dynamic_slice_in_dim(block, (1 - me) * share, share, axis=0)
        keep = lax.dynamic_slice_in_dim(block, me * share, share, axis=0)
        total = keep + lax.ppermute(give, "wave", [(0, 1), (1, 0)])
    else:
        total = lax.psum_scatter(block, "wave", scatter_dimension=0, tiled=True)
    return total.transpose(1, 2, 0, 3).reshape(2, block.shape[2], share * LANES)


def on_device(object_field, probes, patterns, offsets, counts):
    side = probes.shape[-1]
    tables = make_tables(side)
    rim = from_behind(object_field[:, :side, :], "region", -1)
    grad_a, prb_a = patch_call(False, offsets, counts, object_field, (), probes, patterns, tables)
    grad_b, prb_b = patch_call(
        True, offsets, counts, object_field, (rim, grad_a, prb_a), probes, patterns, tables
    )
    arrived = from_behind(grad_b[:, :, side:, :], "region", 1)
    probe_total = lax.psum(prb_b, "region")
    bottom = wave_sum(grad_b[:, :, :side, :])
    top = wave_sum(grad_a[:, :, :side, :] + arrived)
    return (jnp.concatenate([top, bottom], axis=1), probe_total[None])


def solution(mesh):
    in_specs = (
        P(None, "region", None),
        P("wave", None, None, None),
        P("wave", "region", None, None),
        P("region", None),
        P("region"),
    )
    out_specs = (P(None, "region", "wave"), P("wave", None, None, None))
    return jax.shard_map(
        on_device, mesh=mesh, in_specs=in_specs, out_specs=out_specs, check_vma=False
    )
```

```python
import functools
import math

import jax
import jax.numpy as jnp
import numpy as np
from jax import lax
from jax.experimental import pallas as pl
from jax.experimental.pallas import tpu as pltpu
from jax.sharding import PartitionSpec as P

STRIP = 32
LANES = 128
UNROLL = 2
VMEM_LIMIT = 56 * 1024 * 1024


def from_behind(block, axis, distance):
    devices = range(lax.axis_size(axis))
    route = [(i - distance, i) for i in devices if i - distance in devices]
    return lax.ppermute(block, axis, route)


def make_tables(side):
    index = np.arange(side)
    phase = (index[:, None] * index[None, :] % side) * (2.0 * math.pi / side)
    cos = (np.cos(phase) / math.sqrt(side)).astype(np.float32)
    sin = (np.sin(phase) / math.sqrt(side)).astype(np.float32)
    forward = np.block([[cos, sin], [-sin, cos]])
    inverse = np.block([[cos, -sin], [sin, cos]])
    return jnp.asarray(forward, jnp.bfloat16), jnp.asarray(inverse, jnp.bfloat16)


def patch_kernel(second, side, slots, width, *refs):
    offs, count, field, *refs = refs
    if second:
        rim, grad_in, prb_in, *refs = refs
    probe, patterns, forward, inverse = refs[:4]
    grad, prb = refs[4:6]
    ext, pats, order, sems = refs[6:10]
    patch = refs[10 : 10 + UNROLL]
    wave = refs[10 + UNROLL : 10 + 2 * UNROLL]
    half = refs[10 + 2 * UNROLL : 10 + 3 * UNROLL]
    far = refs[10 + 3 * UNROLL : 10 + 4 * UNROLL]
    base = side if second else 0

    copies = [pltpu.make_async_copy(patterns.at[0], pats, sems.at[0])]
    if second:
        copies += [
            pltpu.make_async_copy(
                grad_in.at[:, :, pl.ds(side, side)], grad.at[:, :, pl.ds(0, side)], sems.at[1]
            ),
        ]
    for k in range(width // LANES):
        cols = pl.ds(k * LANES, LANES)
        if second:
            copies += [
                pltpu.make_async_copy(
                    field.at[:, pl.ds(side, side), cols], ext.at[k, :, pl.ds(0, side)], sems.at[2 + 2 * k]
                ),
                pltpu.make_async_copy(
                    rim.at[:, :, cols], ext.at[k, :, pl.ds(side, side)], sems.at[3 + 2 * k]
                ),
            ]
        else:
            copies += [pltpu.make_async_copy(field.at[:, :, cols], ext.at[k], sems.at[2 + 2 * k])]
    for copy in copies:
        copy.start()

    if second:
        grad[:, :, side:, :] = jnp.zeros((width // LANES, 2, side, LANES), jnp.float32)
        prb[...] = prb_in[...]
    else:
        grad[...] = jnp.zeros_like(grad)
        prb[...] = jnp.zeros_like(prb)

    def gather(slot, found):
        row = offs[slot, 0]
        inside = (row >= side) if second else (row < side)
        take = inside & (slot < count[0])

        @pl.when(take)
        def _():
            order[found] = slot

        return found + take.astype(jnp.int32)

    for lane in range(UNROLL):
        order[slots + lane] = 0
    total = lax.fori_loop(0, slots, gather, jnp.int32(0))
    for lane in range(UNROLL):
        order[total + lane] = 0
    for copy in copies:
        copy.wait()

    chunks = side // LANES
    lane_id = lax.broadcasted_iota(jnp.int32, (STRIP, LANES), 1)

    def place(position):
        slot = order[position]
        row = jnp.clip(offs[slot, 0] - base, 0, side - 1)
        col = offs[slot, 1]
        start = jnp.minimum(col // LANES, width // LANES - chunks - 1)
        return slot, row, start, col - start * LANES

    def body(step, carry):
        placed = [place(step * UNROLL + u) for u in range(UNROLL)]
        for u in range(UNROLL):
            slot, row, start, shift = placed[u]
            back_shift = lax.rem(LANES - shift, LANES)
            for s in range(side // STRIP):
                at = slice(s * STRIP, (s + 1) * STRIP)
                parts = []
                for plane in range(2):
                    rolled = [
                        pltpu.roll(
                            ext[start + k, plane, pl.ds(row + s * STRIP, STRIP), :],
                            back_shift,
                            1,
                        )
                        for k in range(chunks + 1)
                    ]
                    parts.append(
                        [
                            jnp.where(lane_id < LANES - shift, rolled[k], rolled[k + 1])
                            for k in range(chunks)
                        ]
                    )
                for k in range(chunks):
                    cols = slice(k * LANES, (k + 1) * LANES)
                    re, im = parts[0][k], parts[1][k]
                    p_re, p_im = probe[0, 0, at, cols], probe[0, 1, at, cols]
                    patch[u][0, at, cols] = re
                    patch[u][1, at, cols] = im
                    wave[u][at, cols] = (p_re * re - p_im * im).astype(jnp.bfloat16)
                    wave[u][side + s * STRIP : side + (s + 1) * STRIP, cols] = (
                        p_re * im + p_im * re
                    ).astype(jnp.bfloat16)
        for u in range(UNROLL):
            product = jnp.dot(forward[...], wave[u][...], preferred_element_type=jnp.float32)
            half[u][:, :side] = product[:side].astype(jnp.bfloat16)
            half[u][:, side:] = product[side:].astype(jnp.bfloat16)
        for u in range(UNROLL):
            far[u][...] = jnp.dot(half[u][...], inverse[...], preferred_element_type=jnp.float32)
        for u in range(UNROLL):
            slot = placed[u][0]
            for s in range(side // STRIP):
                at = slice(s * STRIP, (s + 1) * STRIP)
                f_re, f_im = far[u][at, :side], far[u][at, side:]
                seen = pats[slot, at, :].astype(jnp.float32)
                excess = f_re * f_re + f_im * f_im - seen
                wave[u][at, :] = (excess * f_re).astype(jnp.bfloat16)
                wave[u][side + s * STRIP : side + (s + 1) * STRIP, :] = (excess * f_im).astype(
                    jnp.bfloat16
                )
        for u in range(UNROLL):
            product = jnp.dot(inverse[...], wave[u][...], preferred_element_type=jnp.float32)
            half[u][:, :side] = product[:side].astype(jnp.bfloat16)
            half[u][:, side:] = product[side:].astype(jnp.bfloat16)
        for u in range(UNROLL):
            far[u][...] = jnp.dot(half[u][...], forward[...], preferred_element_type=jnp.float32)
        for u in range(UNROLL):
            slot, row, start, shift = placed[u]
            valid = (step * UNROLL + u < total).astype(jnp.float32)
            for s in range(side // STRIP):
                at = slice(s * STRIP, (s + 1) * STRIP)
                terms = [[], []]
                for k in range(chunks):
                    cols = slice(k * LANES, (k + 1) * LANES)
                    c_re = far[u][at, cols] * valid
                    c_im = far[u][at, side + k * LANES : side + (k + 1) * LANES] * valid
                    re, im = patch[u][0, at, cols], patch[u][1, at, cols]
                    prb[0, at, cols] += re * c_re + im * c_im
                    prb[1, at, cols] += re * c_im - im * c_re
                    p_re, p_im = probe[0, 0, at, cols], probe[0, 1, at, cols]
                    terms[0].append(p_re * c_re + p_im * c_im)
                    terms[1].append(p_re * c_im - p_im * c_re)
                for plane in range(2):
                    rolled = [pltpu.roll(t, lax.rem(shift, LANES), 1) for t in terms[plane]]
                    rolled = [jnp.zeros_like(rolled[0])] + rolled + [jnp.zeros_like(rolled[0])]
                    for k in range(chunks + 1):
                        where = (start + k, plane, pl.ds(row + s * STRIP, STRIP))
                        grad[where] += jnp.where(lane_id >= shift, rolled[k + 1], rolled[k])
        return carry

    lax.fori_loop(0, (total + UNROLL - 1) // UNROLL, body, 0)


def patch_call(second, offsets, counts, field, extra, probes, patterns, tables):
    side = probes.shape[-1]
    slots = offsets.shape[0]
    width = field.shape[2]
    smem = pl.BlockSpec(memory_space=pltpu.SMEM)
    vmem = pl.BlockSpec(memory_space=pltpu.VMEM)
    hbm = pl.BlockSpec(memory_space=pl.ANY)
    specs = [smem, smem, hbm] + ([hbm, hbm, vmem] if second else []) + [vmem, hbm, vmem, vmem]
    scratch = [
        pltpu.VMEM((width // LANES, 2, 2 * side, LANES), jnp.float32),
        pltpu.VMEM((slots, side, side), jnp.bfloat16),
        pltpu.SMEM((slots + UNROLL,), jnp.int32),
        pltpu.SemaphoreType.DMA((2 + 2 * (width // LANES),)),
    ]
    scratch += [pltpu.VMEM((2, side, side), jnp.float32)] * UNROLL
    scratch += [pltpu.VMEM((2 * side, side), jnp.bfloat16)] * UNROLL
    scratch += [pltpu.VMEM((side, 2 * side), jnp.bfloat16)] * UNROLL
    scratch += [pltpu.VMEM((side, 2 * side), jnp.float32)] * UNROLL
    return pl.pallas_call(
        functools.partial(patch_kernel, second, side, slots, width),
        out_shape=(
            jax.ShapeDtypeStruct((width // LANES, 2, 2 * side, LANES), jnp.float32),
            jax.ShapeDtypeStruct((2, side, side), jnp.float32),
        ),
        in_specs=specs,
        out_specs=(vmem, vmem),
        scratch_shapes=scratch,
        compiler_params=pltpu.CompilerParams(vmem_limit_bytes=VMEM_LIMIT),
        cost_estimate=pl.CostEstimate(
            flops=slots * 16 * side**3, bytes_accessed=20 * 1024 * 1024, transcendentals=0
        ),
        name="second_half" if second else "first_half",
    )(offsets, counts, field, *extra, probes, patterns, *tables)


def exchange_kernel(waves, regions, a_ref, b_ref, prb_ref, out, total, *scratch):
    halo, low_in, top_in, top_out, a_top, b_low, acc, full, *rest = scratch
    bits = regions.bit_length() - 1
    stages, (local_sem, halo_send, halo_recv, low_sem, top_send, top_recv, rs_sem, ag_sem) = (
        rest[:bits],
        rest[bits:],
    )
    side = a_top.shape[2]
    share = b_low.shape[0]
    me = lax.axis_index("region")
    wave = lax.axis_index("wave")
    mine, other = wave * share, (1 - wave) * share
    first, last = me == 0, me == regions - 1

    def remote(src, dst, send, recv, axis, target):
        return pltpu.make_async_remote_copy(
            src_ref=src,
            dst_ref=dst,
            send_sem=send,
            recv_sem=recv,
            device_id={axis: target},
            device_id_type=pl.DeviceIdType.MESH,
        )

    def flipped(bit):
        value = lax.rem(me // (1 << bit), 2)
        return value, me + (1 - 2 * value) * (1 << bit)

    locals_ = [
        pltpu.make_async_copy(prb_ref, acc, local_sem.at[0]),
        pltpu.make_async_copy(a_ref.at[:, :, pl.ds(0, side)], a_top, local_sem.at[1]),
        pltpu.make_async_copy(
            b_ref.at[pl.ds(mine, share), :, pl.ds(0, side)], b_low, local_sem.at[2]
        ),
    ]
    for copy in locals_:
        copy.start()

    @pl.when(first)
    def _():
        halo[...] = jnp.zeros_like(halo)

    barrier = pltpu.get_barrier_semaphore()

    def greet(axis, target):
        pl.semaphore_signal(
            barrier, inc=1, device_id={axis: target}, device_id_type=pl.DeviceIdType.MESH
        )

    greet("wave", 1 - wave)
    for bit in range(bits):
        greet("region", flipped(bit)[1])
    greet("region", lax.rem(me + 1, regions))
    greet("region", lax.rem(me + regions - 1, regions))
    pl.semaphore_wait(barrier, 3 + bits)

    def halo_copy(chunk, count, sem):
        return remote(
            b_ref.at[pl.ds(chunk, count), :, pl.ds(side, side)],
            halo.at[pl.ds(chunk, count)],
            halo_send.at[sem],
            halo_recv.at[sem],
            "region",
            lax.rem(me + 1, regions),
        )

    halo_copies = [halo_copy(other + j, 1, j) for j in range(share)] + [halo_copy(mine, share, share)]

    @pl.when(jnp.logical_not(last))
    def _():
        halo_copies[0].start()

    low = remote(
        b_ref.at[pl.ds(other, share), :, pl.ds(0, side)],
        low_in,
        low_sem.at[0],
        low_sem.at[1],
        "wave",
        1 - wave,
    )
    low.start()

    @pl.when(jnp.logical_not(last))
    def _():
        for copy in halo_copies[1:]:
            copy.start()

    for copy in locals_:
        copy.wait()

    start, size = jnp.int32(0), acc.shape[0]
    for bit in range(bits):
        value, target = flipped(bit)
        size //= 2
        give = pl.multiple_of(start + (1 - value) * size, 8)
        start = pl.multiple_of(start + value * size, 8)
        copy = remote(
            acc.at[pl.ds(give, size)],
            stages[bit],
            rs_sem.at[0, bit],
            rs_sem.at[1, bit],
            "region",
            target,
        )
        copy.start()
        copy.wait()
        acc[pl.ds(start, size), :] += stages[bit][...]
    full[pl.ds(start, size), :] = acc[pl.ds(start, size), :]

    tops = []
    for j in range(share):
        pl.when(jnp.logical_not(first))(lambda j=j: halo_copies[j].wait_recv())
        top_out[j] = a_top[other + j] + halo[other + j]
        copy = remote(
            top_out.at[j], top_in.at[j], top_send.at[j], top_recv.at[j], "wave", 1 - wave
        )
        copy.start()
        tops.append(copy)

    for bit in reversed(range(bits)):
        value, target = flipped(bit)
        copy = remote(
            full.at[pl.ds(start, size)],
            full.at[pl.ds(start, size)],
            ag_sem.at[0, bit],
            ag_sem.at[1, bit],
            "region",
            target,
        )
        copy.start()
        copy.wait()
        start = pl.multiple_of(start - value * size, 8)
        size *= 2
    total[...] = full[...]

    pl.when(jnp.logical_not(first))(lambda: halo_copies[share].wait_recv())
    low.wait()
    for j in range(share):
        cols = slice(j * LANES, (j + 1) * LANES)
        out[:, side:, cols] = b_low[j] + low_in[j]
        a_top[mine + j] = a_top[mine + j] + halo[mine + j]
    for j in range(share):
        cols = slice(j * LANES, (j + 1) * LANES)
        tops[j].wait()
        out[:, :side, cols] = a_top[mine + j] + top_in[j]

    @pl.when(jnp.logical_not(last))
    def _():
        for copy in halo_copies:
            copy.wait_send()


def exchange_call(grad_a, grad_b, prb, waves, regions):
    chunks, planes, double, _ = grad_a.shape
    side, share = double // 2, chunks // waves
    bits = regions.bit_length() - 1
    vmem = pl.BlockSpec(memory_space=pltpu.VMEM)
    hbm = pl.BlockSpec(memory_space=pl.ANY)
    f32 = jnp.float32
    rows = planes * side

    def block(count):
        return pltpu.VMEM((count, planes, side, LANES), f32)

    scratch = [block(chunks), block(share), block(share), block(share), block(chunks), block(share)]
    scratch += [pltpu.VMEM((rows, side), f32)] * 2
    scratch += [pltpu.VMEM((rows >> (bit + 1), side), f32) for bit in range(bits)]
    dma = pltpu.SemaphoreType.DMA
    scratch += [dma((3,)), dma((share + 1,)), dma((share + 1,)), dma((2,))]
    scratch += [dma((share,)), dma((share,)), dma((2, bits)), dma((2, bits))]
    return pl.pallas_call(
        functools.partial(exchange_kernel, waves, regions),
        out_shape=(
            jax.ShapeDtypeStruct((planes, double, share * LANES), f32),
            jax.ShapeDtypeStruct((rows, side), f32),
        ),
        in_specs=[hbm, hbm, hbm],
        out_specs=(vmem, vmem),
        scratch_shapes=scratch,
        compiler_params=pltpu.CompilerParams(
            vmem_limit_bytes=VMEM_LIMIT, collective_id=0, has_side_effects=True
        ),
        name="exchange",
    )(grad_a, grad_b, prb.reshape(rows, side))


def wave_sum(block):
    share = block.shape[0] // lax.axis_size("wave")
    total = lax.psum_scatter(block, "wave", scatter_dimension=0, tiled=True)
    return total.transpose(1, 2, 0, 3).reshape(2, block.shape[2], share * LANES)


def on_device(object_field, probes, patterns, offsets, counts):
    side = probes.shape[-1]
    waves, regions = lax.axis_size("wave"), lax.axis_size("region")
    tables = make_tables(side)
    rim = from_behind(object_field[:, :side, :], "region", -1)
    grad_a, prb_a = patch_call(False, offsets, counts, object_field, (), probes, patterns, tables)
    grad_b, prb_b = patch_call(
        True, offsets, counts, object_field, (rim, grad_a, prb_a), probes, patterns, tables
    )
    if waves == 2 and regions & (regions - 1) == 0:
        object_out, probe_total = exchange_call(grad_a, grad_b, prb_b, waves, regions)
        return (object_out, probe_total.reshape((1,) + prb_b.shape))
    arrived = from_behind(grad_b[:, :, side:, :], "region", 1)
    probe_total = lax.psum(prb_b, "region")
    bottom = wave_sum(grad_b[:, :, :side, :])
    top = wave_sum(grad_a[:, :, :side, :] + arrived)
    return (jnp.concatenate([top, bottom], axis=1), probe_total[None])


def solution(mesh):
    in_specs = (
        P(None, "region", None),
        P("wave", None, None, None),
        P("wave", "region", None, None),
        P("region", None),
        P("region"),
    )
    out_specs = (P(None, "region", "wave"), P("wave", None, None, None))
    return jax.shard_map(
        on_device, mesh=mesh, in_specs=in_specs, out_specs=out_specs, check_vma=False
    )
```

```python
import functools
import math

import jax
import jax.numpy as jnp
import numpy as np
from jax import lax
from jax.experimental import pallas as pl
from jax.experimental.pallas import tpu as pltpu
from jax.sharding import PartitionSpec as P

STRIP = 32
LANES = 128
UNROLL = 2
PATCH_VMEM = 28 * 1024 * 1024
EXCHANGE_VMEM = 20 * 1024 * 1024
RIM_VMEM = 8 * 1024 * 1024
PIECES = 4


def from_behind(block, axis, distance):
    devices = range(lax.axis_size(axis))
    route = [(i - distance, i) for i in devices if i - distance in devices]
    return lax.ppermute(block, axis, route)


def make_tables(side):
    index = np.arange(side)
    phase = (index[:, None] * index[None, :] % side) * (2.0 * math.pi / side)
    cos = (np.cos(phase) / math.sqrt(side)).astype(np.float32)
    sin = (np.sin(phase) / math.sqrt(side)).astype(np.float32)
    forward = np.block([[cos, sin], [-sin, cos]])
    inverse = np.block([[cos, -sin], [sin, cos]])
    return jnp.asarray(forward, jnp.bfloat16), jnp.asarray(inverse, jnp.bfloat16)


def patch_kernel(side, tile, slots, width, *refs):
    offs, count, field, rim, *refs = refs
    probe, patterns, forward, inverse = refs[:4]
    grad, prb = refs[4:6]
    ext, pats, order, sems = refs[6:10]
    patch = refs[10 : 10 + UNROLL]
    wave = refs[10 + UNROLL : 10 + 2 * UNROLL]
    half = refs[10 + 2 * UNROLL : 10 + 3 * UNROLL]
    far = refs[10 + 3 * UNROLL : 10 + 4 * UNROLL]

    copies = []
    for k in range(width // LANES):
        cols = pl.ds(k * LANES, LANES)
        copies += [
            pltpu.make_async_copy(field.at[:, :, cols], ext.at[k, :, pl.ds(0, tile)], sems.at[2 * k]),
            pltpu.make_async_copy(rim.at[:, :, cols], ext.at[k, :, pl.ds(tile, side)], sems.at[2 * k + 1]),
        ]
    copies += [pltpu.make_async_copy(patterns.at[0], pats, sems.at[2 * (width // LANES)])]
    for copy in copies:
        copy.start()
    grad[...] = jnp.zeros_like(grad)
    prb[...] = jnp.zeros_like(prb)

    def gather(slot, found):
        take = slot < count[0]

        @pl.when(take)
        def _():
            order[found] = slot

        return found + take.astype(jnp.int32)

    for lane in range(UNROLL):
        order[slots + lane] = 0
    total = lax.fori_loop(0, slots, gather, jnp.int32(0))
    for lane in range(UNROLL):
        order[total + lane] = 0
    for copy in copies:
        copy.wait()

    chunks = side // LANES
    lane_id = lax.broadcasted_iota(jnp.int32, (STRIP, LANES), 1)

    def place(position):
        slot = order[position]
        row = offs[slot, 0]
        col = offs[slot, 1]
        start = jnp.minimum(col // LANES, width // LANES - chunks - 1)
        return slot, row, start, col - start * LANES

    def body(step, carry):
        placed = [place(step * UNROLL + u) for u in range(UNROLL)]
        for u in range(UNROLL):
            slot, row, start, shift = placed[u]
            back_shift = lax.rem(LANES - shift, LANES)
            for s in range(side // STRIP):
                at = slice(s * STRIP, (s + 1) * STRIP)
                parts = []
                for plane in range(2):
                    rolled = [
                        pltpu.roll(
                            ext[start + k, plane, pl.ds(row + s * STRIP, STRIP), :],
                            back_shift,
                            1,
                        )
                        for k in range(chunks + 1)
                    ]
                    parts.append(
                        [
                            jnp.where(lane_id < LANES - shift, rolled[k], rolled[k + 1])
                            for k in range(chunks)
                        ]
                    )
                for k in range(chunks):
                    cols = slice(k * LANES, (k + 1) * LANES)
                    re, im = parts[0][k], parts[1][k]
                    p_re, p_im = probe[0, 0, at, cols], probe[0, 1, at, cols]
                    patch[u][0, at, cols] = re
                    patch[u][1, at, cols] = im
                    wave[u][at, cols] = (p_re * re - p_im * im).astype(jnp.bfloat16)
                    wave[u][side + s * STRIP : side + (s + 1) * STRIP, cols] = (
                        p_re * im + p_im * re
                    ).astype(jnp.bfloat16)
        for u in range(UNROLL):
            product = jnp.dot(forward[...], wave[u][...], preferred_element_type=jnp.float32)
            half[u][:, :side] = product[:side].astype(jnp.bfloat16)
            half[u][:, side:] = product[side:].astype(jnp.bfloat16)
        for u in range(UNROLL):
            far[u][...] = jnp.dot(half[u][...], inverse[...], preferred_element_type=jnp.float32)
        for u in range(UNROLL):
            slot = placed[u][0]
            for s in range(side // STRIP):
                at = slice(s * STRIP, (s + 1) * STRIP)
                f_re, f_im = far[u][at, :side], far[u][at, side:]
                seen = pats[slot, at, :].astype(jnp.float32)
                excess = f_re * f_re + f_im * f_im - seen
                wave[u][at, :] = (excess * f_re).astype(jnp.bfloat16)
                wave[u][side + s * STRIP : side + (s + 1) * STRIP, :] = (excess * f_im).astype(
                    jnp.bfloat16
                )
        for u in range(UNROLL):
            product = jnp.dot(inverse[...], wave[u][...], preferred_element_type=jnp.float32)
            half[u][:, :side] = product[:side].astype(jnp.bfloat16)
            half[u][:, side:] = product[side:].astype(jnp.bfloat16)
        for u in range(UNROLL):
            far[u][...] = jnp.dot(half[u][...], forward[...], preferred_element_type=jnp.float32)
        for u in range(UNROLL):
            slot, row, start, shift = placed[u]
            valid = (step * UNROLL + u < total).astype(jnp.float32)
            for s in range(side // STRIP):
                at = slice(s * STRIP, (s + 1) * STRIP)
                terms = [[], []]
                for k in range(chunks):
                    cols = slice(k * LANES, (k + 1) * LANES)
                    c_re = far[u][at, cols] * valid
                    c_im = far[u][at, side + k * LANES : side + (k + 1) * LANES] * valid
                    re, im = patch[u][0, at, cols], patch[u][1, at, cols]
                    prb[0, at, cols] += re * c_re + im * c_im
                    prb[1, at, cols] += re * c_im - im * c_re
                    p_re, p_im = probe[0, 0, at, cols], probe[0, 1, at, cols]
                    terms[0].append(p_re * c_re + p_im * c_im)
                    terms[1].append(p_re * c_im - p_im * c_re)
                for plane in range(2):
                    rolled = [pltpu.roll(t, lax.rem(shift, LANES), 1) for t in terms[plane]]
                    rolled = [jnp.zeros_like(rolled[0])] + rolled + [jnp.zeros_like(rolled[0])]
                    for k in range(chunks + 1):
                        where = (start + k, plane, pl.ds(row + s * STRIP, STRIP))
                        grad[where] += jnp.where(lane_id >= shift, rolled[k + 1], rolled[k])
        return carry

    lax.fori_loop(0, (total + UNROLL - 1) // UNROLL, body, 0)


def patch_call(offsets, counts, field, rim, probes, patterns, tables):
    side = probes.shape[-1]
    slots = offsets.shape[0]
    tile, width = field.shape[1:]
    smem = pl.BlockSpec(memory_space=pltpu.SMEM)
    vmem = pl.BlockSpec(memory_space=pltpu.VMEM)
    hbm = pl.BlockSpec(memory_space=pl.ANY)
    specs = [smem, smem, hbm, hbm, vmem, hbm, vmem, vmem]
    scratch = [
        pltpu.VMEM((width // LANES, 2, tile + side, LANES), jnp.float32),
        pltpu.VMEM((slots, side, side), jnp.bfloat16),
        pltpu.SMEM((slots + UNROLL,), jnp.int32),
        pltpu.SemaphoreType.DMA((1 + 2 * (width // LANES),)),
    ]
    scratch += [pltpu.VMEM((2, side, side), jnp.float32)] * UNROLL
    scratch += [pltpu.VMEM((2 * side, side), jnp.bfloat16)] * UNROLL
    scratch += [pltpu.VMEM((side, 2 * side), jnp.bfloat16)] * UNROLL
    scratch += [pltpu.VMEM((side, 2 * side), jnp.float32)] * UNROLL
    return pl.pallas_call(
        functools.partial(patch_kernel, side, tile, slots, width),
        out_shape=(
            jax.ShapeDtypeStruct((width // LANES, 2, tile + side, LANES), jnp.float32),
            jax.ShapeDtypeStruct((2, side, side), jnp.float32),
        ),
        in_specs=specs,
        out_specs=(vmem, vmem),
        scratch_shapes=scratch,
        compiler_params=pltpu.CompilerParams(vmem_limit_bytes=PATCH_VMEM),
        cost_estimate=pl.CostEstimate(
            flops=slots * 16 * side**3, bytes_accessed=20 * 1024 * 1024, transcendentals=0
        ),
        name="patches",
    )(offsets, counts, field, rim, probes, patterns, *tables)


def exchange_kernel(regions, grad_ref, prb_ref, out, total, *scratch):
    halo, low_in, top_in, top_out, a_top, b_low, acc, full, *rest = scratch
    bits = regions.bit_length() - 1
    stages, (local_sem, halo_send, halo_recv, low_sem, top_send, top_recv, rs_sem, ag_sem) = (
        rest[:bits],
        rest[bits:],
    )
    side = a_top.shape[2]
    tile = grad_ref.shape[2] - side
    share = b_low.shape[0]
    me = lax.axis_index("region")
    wave = lax.axis_index("wave")
    mine, other = wave * share, (1 - wave) * share
    first, last = me == 0, me == regions - 1

    def remote(src, dst, send, recv, axis, target):
        return pltpu.make_async_remote_copy(
            src_ref=src,
            dst_ref=dst,
            send_sem=send,
            recv_sem=recv,
            device_id={axis: target},
            device_id_type=pl.DeviceIdType.MESH,
        )

    def flipped(bit):
        value = lax.rem(me // (1 << bit), 2)
        return value, me + (1 - 2 * value) * (1 << bit)

    locals_ = [
        pltpu.make_async_copy(prb_ref, acc, local_sem.at[0]),
        pltpu.make_async_copy(grad_ref.at[:, :, pl.ds(0, side)], a_top, local_sem.at[1]),
        pltpu.make_async_copy(
            grad_ref.at[pl.ds(mine, share), :, pl.ds(side, tile - side)], b_low, local_sem.at[2]
        ),
    ]
    for copy in locals_:
        copy.start()

    @pl.when(first)
    def _():
        halo[...] = jnp.zeros_like(halo)

    barrier = pltpu.get_barrier_semaphore()

    def greet(axis, target):
        pl.semaphore_signal(
            barrier, inc=1, device_id={axis: target}, device_id_type=pl.DeviceIdType.MESH
        )

    greet("wave", 1 - wave)
    for bit in range(bits):
        greet("region", flipped(bit)[1])
    greet("region", lax.rem(me + 1, regions))
    greet("region", lax.rem(me + regions - 1, regions))
    pl.semaphore_wait(barrier, 3 + bits)

    def halo_copy(chunk, count, sem):
        return remote(
            grad_ref.at[pl.ds(chunk, count), :, pl.ds(tile, side)],
            halo.at[pl.ds(chunk, count)],
            halo_send.at[sem],
            halo_recv.at[sem],
            "region",
            lax.rem(me + 1, regions),
        )

    halo_copies = [halo_copy(other + j, 1, j) for j in range(share)] + [halo_copy(mine, share, share)]

    @pl.when(jnp.logical_not(last))
    def _():
        halo_copies[0].start()

    low = remote(
        grad_ref.at[pl.ds(other, share), :, pl.ds(side, tile - side)],
        low_in,
        low_sem.at[0],
        low_sem.at[1],
        "wave",
        1 - wave,
    )
    low.start()

    @pl.when(jnp.logical_not(last))
    def _():
        for copy in halo_copies[1:]:
            copy.start()

    for copy in locals_:
        copy.wait()

    start, size = jnp.int32(0), acc.shape[0]
    for bit in range(bits):
        value, target = flipped(bit)
        size //= 2
        give = pl.multiple_of(start + (1 - value) * size, 8)
        start = pl.multiple_of(start + value * size, 8)
        copy = remote(
            acc.at[pl.ds(give, size)],
            stages[bit],
            rs_sem.at[0, bit],
            rs_sem.at[1, bit],
            "region",
            target,
        )
        copy.start()
        copy.wait()
        acc[pl.ds(start, size), :] += stages[bit][...]
    full[pl.ds(start, size), :] = acc[pl.ds(start, size), :]

    tops = []
    for j in range(share):
        pl.when(jnp.logical_not(first))(lambda j=j: halo_copies[j].wait_recv())
        top_out[j] = a_top[other + j] + halo[other + j]
        copy = remote(
            top_out.at[j], top_in.at[j], top_send.at[j], top_recv.at[j], "wave", 1 - wave
        )
        copy.start()
        tops.append(copy)

    for bit in reversed(range(bits)):
        value, target = flipped(bit)
        copy = remote(
            full.at[pl.ds(start, size)],
            full.at[pl.ds(start, size)],
            ag_sem.at[0, bit],
            ag_sem.at[1, bit],
            "region",
            target,
        )
        copy.start()
        copy.wait()
        start = pl.multiple_of(start - value * size, 8)
        size *= 2
    total[...] = full[...]

    pl.when(jnp.logical_not(first))(lambda: halo_copies[share].wait_recv())
    low.wait()
    for j in range(share):
        cols = slice(j * LANES, (j + 1) * LANES)
        out[:, side:, cols] = b_low[j] + low_in[j]
        a_top[mine + j] = a_top[mine + j] + halo[mine + j]
    for j in range(share):
        cols = slice(j * LANES, (j + 1) * LANES)
        tops[j].wait()
        out[:, :side, cols] = a_top[mine + j] + top_in[j]

    @pl.when(jnp.logical_not(last))
    def _():
        for copy in halo_copies:
            copy.wait_send()


def exchange_call(grad, prb, waves, regions):
    chunks, planes, all_rows, _ = grad.shape
    side, share = prb.shape[-1], chunks // waves
    tile = all_rows - side
    bits = regions.bit_length() - 1
    vmem = pl.BlockSpec(memory_space=pltpu.VMEM)
    hbm = pl.BlockSpec(memory_space=pl.ANY)
    f32 = jnp.float32
    rows = planes * side

    def block(count, height):
        return pltpu.VMEM((count, planes, height, LANES), f32)

    scratch = [block(chunks, side), block(share, tile - side), block(share, side)]
    scratch += [block(share, side), block(chunks, side), block(share, tile - side)]
    scratch += [pltpu.VMEM((rows, side), f32)] * 2
    scratch += [pltpu.VMEM((rows >> (bit + 1), side), f32) for bit in range(bits)]
    dma = pltpu.SemaphoreType.DMA
    scratch += [dma((3,)), dma((share + 1,)), dma((share + 1,)), dma((2,))]
    scratch += [dma((share,)), dma((share,)), dma((2, bits)), dma((2, bits))]
    return pl.pallas_call(
        functools.partial(exchange_kernel, regions),
        out_shape=(
            jax.ShapeDtypeStruct((planes, tile, share * LANES), f32),
            jax.ShapeDtypeStruct((rows, side), f32),
        ),
        in_specs=[hbm, hbm],
        out_specs=(vmem, vmem),
        scratch_shapes=scratch,
        compiler_params=pltpu.CompilerParams(
            vmem_limit_bytes=EXCHANGE_VMEM, collective_id=0, has_side_effects=True
        ),
        name="exchange",
    )(grad, prb.reshape(rows, side))


def wave_sum(block):
    share = block.shape[0] // lax.axis_size("wave")
    total = lax.psum_scatter(block, "wave", scatter_dimension=0, tiled=True)
    return total.transpose(1, 2, 0, 3).reshape(2, block.shape[2], share * LANES)


def rim_kernel(regions, field, rim, sems):
    side = rim.shape[1]
    me, wave = lax.axis_index("region"), lax.axis_index("wave")
    first, last = me == 0, me == regions - 1
    odd = lax.rem(me, 2) == 1
    behind, ahead = lax.rem(me + regions - 1, regions), lax.rem(me + 1, regions)
    part = side // PIECES

    @pl.when(last)
    def _():
        rim[...] = jnp.zeros_like(rim)

    barrier = pltpu.get_barrier_semaphore()
    for target in ({"wave": 1 - wave}, {"region": behind}, {"region": ahead}):
        pl.semaphore_signal(
            barrier, inc=1, device_id=target, device_id_type=pl.DeviceIdType.MESH
        )
    pl.semaphore_wait(barrier, 3)

    def remote(src, dst, row, index, target):
        return pltpu.make_async_remote_copy(
            src_ref=src,
            dst_ref=dst,
            send_sem=sems.at[row, index],
            recv_sem=sems.at[row + 1, index],
            device_id=target,
            device_id_type=pl.DeviceIdType.MESH,
        )

    whole = remote(field.at[:, pl.ds(0, side)], rim, 0, PIECES, {"region": behind})
    pieces = [
        remote(
            field.at[wave, pl.ds(j * part, part)],
            rim.at[wave, pl.ds(j * part, part)],
            0,
            j,
            {"region": behind},
        )
        for j in range(PIECES)
    ]
    relays = [
        remote(
            rim.at[wave, pl.ds(j * part, part)],
            rim.at[wave, pl.ds(j * part, part)],
            2,
            j,
            {"wave": 1 - wave},
        )
        for j in range(PIECES)
    ]
    sends_pieces = jnp.logical_not(odd) & jnp.logical_not(first)
    relaying = odd & jnp.logical_not(last)

    @pl.when(odd)
    def _():
        whole.start()

    @pl.when(sends_pieces)
    def _():
        for piece in pieces:
            piece.start()

    @pl.when(relaying)
    def _():
        for piece, relay in zip(pieces, relays):
            piece.wait_recv()
            relay.start()
        for relay in relays:
            relay.wait()

    @pl.when(jnp.logical_not(odd))
    def _():
        whole.wait_recv()

    @pl.when(odd)
    def _():
        whole.wait_send()

    @pl.when(sends_pieces)
    def _():
        for piece in pieces:
            piece.wait_send()


def rim_call(field, side, regions):
    return pl.pallas_call(
        functools.partial(rim_kernel, regions),
        out_shape=jax.ShapeDtypeStruct((field.shape[0], side, field.shape[2]), jnp.float32),
        in_specs=[pl.BlockSpec(memory_space=pl.ANY)],
        out_specs=pl.BlockSpec(memory_space=pltpu.VMEM),
        scratch_shapes=[pltpu.SemaphoreType.DMA((4, PIECES + 1))],
        compiler_params=pltpu.CompilerParams(
            vmem_limit_bytes=RIM_VMEM, collective_id=1, has_side_effects=True
        ),
        name="rim",
    )(field)


def on_device(object_field, probes, patterns, offsets, counts):
    side = probes.shape[-1]
    tile = object_field.shape[1]
    waves, regions = lax.axis_size("wave"), lax.axis_size("region")
    paired = waves == 2 and regions & (regions - 1) == 0
    tables = make_tables(side)
    if paired:
        rim = rim_call(object_field, side, regions)
    else:
        rim = from_behind(object_field[:, :side, :], "region", -1)
    grad, prb = patch_call(offsets, counts, object_field, rim, probes, patterns, tables)
    if paired:
        object_out, probe_total = exchange_call(grad, prb, waves, regions)
        return (object_out, probe_total.reshape((1,) + prb.shape))
    arrived = from_behind(grad[:, :, tile:, :], "region", 1)
    probe_total = lax.psum(prb, "region")
    bottom = wave_sum(grad[:, :, side:tile, :])
    top = wave_sum(grad[:, :, :side, :] + arrived)
    return (jnp.concatenate([top, bottom], axis=1), probe_total[None])


def solution(mesh):
    in_specs = (
        P(None, "region", None),
        P("wave", None, None, None),
        P("wave", "region", None, None),
        P("region", None),
        P("region"),
    )
    out_specs = (P(None, "region", "wave"), P("wave", None, None, None))
    return jax.shard_map(
        on_device, mesh=mesh, in_specs=in_specs, out_specs=out_specs, check_vma=False
    )
```

```python
import functools
import math

import jax
import jax.numpy as jnp
import numpy as np
from jax import lax
from jax.experimental import pallas as pl
from jax.experimental.pallas import tpu as pltpu
from jax.sharding import PartitionSpec as P

STRIP = 32
LANES = 128
UNROLL = 2
PATCH_VMEM = 28 * 1024 * 1024
EXCHANGE_VMEM = 20 * 1024 * 1024
RIM_VMEM = 8 * 1024 * 1024
PIECES = 8


def from_behind(block, axis, distance):
    devices = range(lax.axis_size(axis))
    route = [(i - distance, i) for i in devices if i - distance in devices]
    return lax.ppermute(block, axis, route)


def make_tables(side):
    index = np.arange(side)
    phase = (index[:, None] * index[None, :] % side) * (2.0 * math.pi / side)
    cos = (np.cos(phase) / math.sqrt(side)).astype(np.float32)
    sin = (np.sin(phase) / math.sqrt(side)).astype(np.float32)
    forward = np.block([[cos, sin], [-sin, cos]])
    inverse = np.block([[cos, -sin], [sin, cos]])
    return jnp.asarray(forward, jnp.bfloat16), jnp.asarray(inverse, jnp.bfloat16)


def patch_kernel(side, tile, slots, width, *refs):
    offs, count, field, rim, *refs = refs
    probe, patterns, forward, inverse = refs[:4]
    grad, prb = refs[4:6]
    ext, pats, order, sems = refs[6:10]
    patch = refs[10 : 10 + UNROLL]
    wave = refs[10 + UNROLL : 10 + 2 * UNROLL]
    half = refs[10 + 2 * UNROLL : 10 + 3 * UNROLL]
    far = refs[10 + 3 * UNROLL : 10 + 4 * UNROLL]

    copies = []
    for k in range(width // LANES):
        cols = pl.ds(k * LANES, LANES)
        copies += [
            pltpu.make_async_copy(field.at[:, :, cols], ext.at[k, :, pl.ds(0, tile)], sems.at[2 * k]),
            pltpu.make_async_copy(rim.at[:, :, cols], ext.at[k, :, pl.ds(tile, side)], sems.at[2 * k + 1]),
        ]
    copies += [pltpu.make_async_copy(patterns.at[0], pats, sems.at[2 * (width // LANES)])]
    for copy in copies:
        copy.start()
    grad[...] = jnp.zeros_like(grad)
    prb[...] = jnp.zeros_like(prb)

    def gather(slot, found):
        take = slot < count[0]

        @pl.when(take)
        def _():
            order[found] = slot

        return found + take.astype(jnp.int32)

    for lane in range(UNROLL):
        order[slots + lane] = 0
    total = lax.fori_loop(0, slots, gather, jnp.int32(0))
    for lane in range(UNROLL):
        order[total + lane] = 0
    for copy in copies:
        copy.wait()

    chunks = side // LANES
    lane_id = lax.broadcasted_iota(jnp.int32, (STRIP, LANES), 1)

    def place(position):
        slot = order[position]
        row = offs[slot, 0]
        col = offs[slot, 1]
        start = jnp.minimum(col // LANES, width // LANES - chunks - 1)
        return slot, row, start, col - start * LANES

    def body(step, carry):
        placed = [place(step * UNROLL + u) for u in range(UNROLL)]
        for u in range(UNROLL):
            slot, row, start, shift = placed[u]
            back_shift = lax.rem(LANES - shift, LANES)
            for s in range(side // STRIP):
                at = slice(s * STRIP, (s + 1) * STRIP)
                parts = []
                for plane in range(2):
                    rolled = [
                        pltpu.roll(
                            ext[start + k, plane, pl.ds(row + s * STRIP, STRIP), :],
                            back_shift,
                            1,
                        )
                        for k in range(chunks + 1)
                    ]
                    parts.append(
                        [
                            jnp.where(lane_id < LANES - shift, rolled[k], rolled[k + 1])
                            for k in range(chunks)
                        ]
                    )
                for k in range(chunks):
                    cols = slice(k * LANES, (k + 1) * LANES)
                    re, im = parts[0][k], parts[1][k]
                    p_re, p_im = probe[0, 0, at, cols], probe[0, 1, at, cols]
                    patch[u][0, at, cols] = re
                    patch[u][1, at, cols] = im
                    wave[u][at, cols] = (p_re * re - p_im * im).astype(jnp.bfloat16)
                    wave[u][side + s * STRIP : side + (s + 1) * STRIP, cols] = (
                        p_re * im + p_im * re
                    ).astype(jnp.bfloat16)
        for u in range(UNROLL):
            product = jnp.dot(forward[...], wave[u][...], preferred_element_type=jnp.float32)
            half[u][:, :side] = product[:side].astype(jnp.bfloat16)
            half[u][:, side:] = product[side:].astype(jnp.bfloat16)
        for u in range(UNROLL):
            far[u][...] = jnp.dot(half[u][...], inverse[...], preferred_element_type=jnp.float32)
        for u in range(UNROLL):
            slot = placed[u][0]
            for s in range(side // STRIP):
                at = slice(s * STRIP, (s + 1) * STRIP)
                f_re, f_im = far[u][at, :side], far[u][at, side:]
                seen = pats[slot, at, :].astype(jnp.float32)
                excess = f_re * f_re + f_im * f_im - seen
                wave[u][at, :] = (excess * f_re).astype(jnp.bfloat16)
                wave[u][side + s * STRIP : side + (s + 1) * STRIP, :] = (excess * f_im).astype(
                    jnp.bfloat16
                )
        for u in range(UNROLL):
            product = jnp.dot(inverse[...], wave[u][...], preferred_element_type=jnp.float32)
            half[u][:, :side] = product[:side].astype(jnp.bfloat16)
            half[u][:, side:] = product[side:].astype(jnp.bfloat16)
        for u in range(UNROLL):
            far[u][...] = jnp.dot(half[u][...], forward[...], preferred_element_type=jnp.float32)
        for u in range(UNROLL):
            slot, row, start, shift = placed[u]
            valid = (step * UNROLL + u < total).astype(jnp.float32)
            for s in range(side // STRIP):
                at = slice(s * STRIP, (s + 1) * STRIP)
                terms = [[], []]
                for k in range(chunks):
                    cols = slice(k * LANES, (k + 1) * LANES)
                    c_re = far[u][at, cols] * valid
                    c_im = far[u][at, side + k * LANES : side + (k + 1) * LANES] * valid
                    re, im = patch[u][0, at, cols], patch[u][1, at, cols]
                    prb[0, at, cols] += re * c_re + im * c_im
                    prb[1, at, cols] += re * c_im - im * c_re
                    p_re, p_im = probe[0, 0, at, cols], probe[0, 1, at, cols]
                    terms[0].append(p_re * c_re + p_im * c_im)
                    terms[1].append(p_re * c_im - p_im * c_re)
                for plane in range(2):
                    rolled = [pltpu.roll(t, lax.rem(shift, LANES), 1) for t in terms[plane]]
                    rolled = [jnp.zeros_like(rolled[0])] + rolled + [jnp.zeros_like(rolled[0])]
                    for k in range(chunks + 1):
                        where = (start + k, plane, pl.ds(row + s * STRIP, STRIP))
                        grad[where] += jnp.where(lane_id >= shift, rolled[k + 1], rolled[k])
        return carry

    lax.fori_loop(0, (total + UNROLL - 1) // UNROLL, body, 0)


def patch_call(offsets, counts, field, rim, probes, patterns, tables):
    side = probes.shape[-1]
    slots = offsets.shape[0]
    tile, width = field.shape[1:]
    smem = pl.BlockSpec(memory_space=pltpu.SMEM)
    vmem = pl.BlockSpec(memory_space=pltpu.VMEM)
    hbm = pl.BlockSpec(memory_space=pl.ANY)
    specs = [smem, smem, hbm, hbm, vmem, hbm, vmem, vmem]
    scratch = [
        pltpu.VMEM((width // LANES, 2, tile + side, LANES), jnp.float32),
        pltpu.VMEM((slots, side, side), jnp.bfloat16),
        pltpu.SMEM((slots + UNROLL,), jnp.int32),
        pltpu.SemaphoreType.DMA((1 + 2 * (width // LANES),)),
    ]
    scratch += [pltpu.VMEM((2, side, side), jnp.float32)] * UNROLL
    scratch += [pltpu.VMEM((2 * side, side), jnp.bfloat16)] * UNROLL
    scratch += [pltpu.VMEM((side, 2 * side), jnp.bfloat16)] * UNROLL
    scratch += [pltpu.VMEM((side, 2 * side), jnp.float32)] * UNROLL
    return pl.pallas_call(
        functools.partial(patch_kernel, side, tile, slots, width),
        out_shape=(
            jax.ShapeDtypeStruct((width // LANES, 2, tile + side, LANES), jnp.float32),
            jax.ShapeDtypeStruct((2, side, side), jnp.float32),
        ),
        in_specs=specs,
        out_specs=(vmem, vmem),
        scratch_shapes=scratch,
        compiler_params=pltpu.CompilerParams(vmem_limit_bytes=PATCH_VMEM),
        cost_estimate=pl.CostEstimate(
            flops=slots * 16 * side**3, bytes_accessed=20 * 1024 * 1024, transcendentals=0
        ),
        name="patches",
    )(offsets, counts, field, rim, probes, patterns, *tables)


def exchange_kernel(regions, grad_ref, prb_ref, out, total, *scratch):
    halo, low_in, top_in, top_out, a_top, b_low, acc, full, *rest = scratch
    bits = regions.bit_length() - 1
    stages, (local_sem, halo_send, halo_recv, low_sem, top_send, top_recv, rs_sem, ag_sem) = (
        rest[:bits],
        rest[bits:],
    )
    side = a_top.shape[2]
    tile = grad_ref.shape[2] - side
    share = b_low.shape[0]
    me = lax.axis_index("region")
    wave = lax.axis_index("wave")
    mine, other = wave * share, (1 - wave) * share
    first, last = me == 0, me == regions - 1

    def remote(src, dst, send, recv, axis, target):
        return pltpu.make_async_remote_copy(
            src_ref=src,
            dst_ref=dst,
            send_sem=send,
            recv_sem=recv,
            device_id={axis: target},
            device_id_type=pl.DeviceIdType.MESH,
        )

    def flipped(bit):
        value = lax.rem(me // (1 << bit), 2)
        return value, me + (1 - 2 * value) * (1 << bit)

    locals_ = [
        pltpu.make_async_copy(prb_ref, acc, local_sem.at[0]),
        pltpu.make_async_copy(grad_ref.at[:, :, pl.ds(0, side)], a_top, local_sem.at[1]),
        pltpu.make_async_copy(
            grad_ref.at[pl.ds(mine, share), :, pl.ds(side, tile - side)], b_low, local_sem.at[2]
        ),
    ]
    for copy in locals_:
        copy.start()

    @pl.when(first)
    def _():
        halo[...] = jnp.zeros_like(halo)

    barrier = pltpu.get_barrier_semaphore()

    def greet(axis, target):
        pl.semaphore_signal(
            barrier, inc=1, device_id={axis: target}, device_id_type=pl.DeviceIdType.MESH
        )

    greet("wave", 1 - wave)
    for bit in range(bits):
        greet("region", flipped(bit)[1])
    greet("region", lax.rem(me + 1, regions))
    greet("region", lax.rem(me + regions - 1, regions))
    pl.semaphore_wait(barrier, 3 + bits)

    def halo_copy(chunk, count, sem):
        return remote(
            grad_ref.at[pl.ds(chunk, count), :, pl.ds(tile, side)],
            halo.at[pl.ds(chunk, count)],
            halo_send.at[sem],
            halo_recv.at[sem],
            "region",
            lax.rem(me + 1, regions),
        )

    halo_copies = [halo_copy(other + j, 1, j) for j in range(share)] + [halo_copy(mine, share, share)]

    @pl.when(jnp.logical_not(last))
    def _():
        halo_copies[0].start()

    low = remote(
        grad_ref.at[pl.ds(other, share), :, pl.ds(side, tile - side)],
        low_in,
        low_sem.at[0],
        low_sem.at[1],
        "wave",
        1 - wave,
    )
    low.start()

    @pl.when(jnp.logical_not(last))
    def _():
        for copy in halo_copies[1:share]:
            copy.start()

    for copy in locals_:
        copy.wait()

    tops = []
    for j in range(share):
        pl.when(jnp.logical_not(first))(lambda j=j: halo_copies[j].wait_recv())
        top_out[j] = a_top[other + j] + halo[other + j]
        copy = remote(
            top_out.at[j], top_in.at[j], top_send.at[j], top_recv.at[j], "wave", 1 - wave
        )
        copy.start()
        tops.append(copy)

    @pl.when(jnp.logical_not(last))
    def _():
        halo_copies[share].start()

    start, size = jnp.int32(0), acc.shape[0]
    for bit in range(bits):
        value, target = flipped(bit)
        size //= 2
        give = pl.multiple_of(start + (1 - value) * size, 8)
        start = pl.multiple_of(start + value * size, 8)
        copy = remote(
            acc.at[pl.ds(give, size)],
            stages[bit],
            rs_sem.at[0, bit],
            rs_sem.at[1, bit],
            "region",
            target,
        )
        copy.start()
        copy.wait()
        acc[pl.ds(start, size), :] += stages[bit][...]
    full[pl.ds(start, size), :] = acc[pl.ds(start, size), :]

    for bit in reversed(range(bits)):
        value, target = flipped(bit)
        copy = remote(
            full.at[pl.ds(start, size)],
            full.at[pl.ds(start, size)],
            ag_sem.at[0, bit],
            ag_sem.at[1, bit],
            "region",
            target,
        )
        copy.start()
        copy.wait()
        start = pl.multiple_of(start - value * size, 8)
        size *= 2
    total[...] = full[...]

    pl.when(jnp.logical_not(first))(lambda: halo_copies[share].wait_recv())
    low.wait()
    for j in range(share):
        cols = slice(j * LANES, (j + 1) * LANES)
        out[:, side:, cols] = b_low[j] + low_in[j]
        a_top[mine + j] = a_top[mine + j] + halo[mine + j]
    for j in range(share):
        cols = slice(j * LANES, (j + 1) * LANES)
        tops[j].wait()
        out[:, :side, cols] = a_top[mine + j] + top_in[j]

    @pl.when(jnp.logical_not(last))
    def _():
        for copy in halo_copies:
            copy.wait_send()


def exchange_call(grad, prb, waves, regions):
    chunks, planes, all_rows, _ = grad.shape
    side, share = prb.shape[-1], chunks // waves
    tile = all_rows - side
    bits = regions.bit_length() - 1
    vmem = pl.BlockSpec(memory_space=pltpu.VMEM)
    hbm = pl.BlockSpec(memory_space=pl.ANY)
    f32 = jnp.float32
    rows = planes * side

    def block(count, height):
        return pltpu.VMEM((count, planes, height, LANES), f32)

    scratch = [block(chunks, side), block(share, tile - side), block(share, side)]
    scratch += [block(share, side), block(chunks, side), block(share, tile - side)]
    scratch += [pltpu.VMEM((rows, side), f32)] * 2
    scratch += [pltpu.VMEM((rows >> (bit + 1), side), f32) for bit in range(bits)]
    dma = pltpu.SemaphoreType.DMA
    scratch += [dma((3,)), dma((share + 1,)), dma((share + 1,)), dma((2,))]
    scratch += [dma((share,)), dma((share,)), dma((2, bits)), dma((2, bits))]
    return pl.pallas_call(
        functools.partial(exchange_kernel, regions),
        out_shape=(
            jax.ShapeDtypeStruct((planes, tile, share * LANES), f32),
            jax.ShapeDtypeStruct((rows, side), f32),
        ),
        in_specs=[hbm, hbm],
        out_specs=(vmem, vmem),
        scratch_shapes=scratch,
        compiler_params=pltpu.CompilerParams(
            vmem_limit_bytes=EXCHANGE_VMEM, collective_id=0, has_side_effects=True
        ),
        name="exchange",
    )(grad, prb.reshape(rows, side))


def wave_sum(block):
    share = block.shape[0] // lax.axis_size("wave")
    total = lax.psum_scatter(block, "wave", scatter_dimension=0, tiled=True)
    return total.transpose(1, 2, 0, 3).reshape(2, block.shape[2], share * LANES)


def rim_kernel(regions, field, rim, sems):
    side = rim.shape[1]
    me, wave = lax.axis_index("region"), lax.axis_index("wave")
    first, last = me == 0, me == regions - 1
    odd = lax.rem(me, 2) == 1
    behind, ahead = lax.rem(me + regions - 1, regions), lax.rem(me + 1, regions)
    part = side // PIECES

    @pl.when(last)
    def _():
        rim[...] = jnp.zeros_like(rim)

    barrier = pltpu.get_barrier_semaphore()
    for target in ({"wave": 1 - wave}, {"region": behind}, {"region": ahead}):
        pl.semaphore_signal(
            barrier, inc=1, device_id=target, device_id_type=pl.DeviceIdType.MESH
        )
    pl.semaphore_wait(barrier, 3)

    def remote(src, dst, row, index, target):
        return pltpu.make_async_remote_copy(
            src_ref=src,
            dst_ref=dst,
            send_sem=sems.at[row, index],
            recv_sem=sems.at[row + 1, index],
            device_id=target,
            device_id_type=pl.DeviceIdType.MESH,
        )

    whole = remote(field.at[:, pl.ds(0, side)], rim, 0, PIECES, {"region": behind})
    pieces = [
        remote(
            field.at[wave, pl.ds(j * part, part)],
            rim.at[wave, pl.ds(j * part, part)],
            0,
            j,
            {"region": behind},
        )
        for j in range(PIECES)
    ]
    relays = [
        remote(
            rim.at[wave, pl.ds(j * part, part)],
            rim.at[wave, pl.ds(j * part, part)],
            2,
            j,
            {"wave": 1 - wave},
        )
        for j in range(PIECES)
    ]
    sends_pieces = jnp.logical_not(odd) & jnp.logical_not(first)
    relaying = odd & jnp.logical_not(last)

    @pl.when(odd)
    def _():
        whole.start()

    @pl.when(sends_pieces)
    def _():
        for j, piece in enumerate(pieces):
            if j >= 2:
                pieces[j - 2].wait_send()
            piece.start()

    @pl.when(relaying)
    def _():
        for piece, relay in zip(pieces, relays):
            piece.wait_recv()
            relay.start()
        for relay in relays:
            relay.wait()

    @pl.when(jnp.logical_not(odd))
    def _():
        whole.wait_recv()

    @pl.when(odd)
    def _():
        whole.wait_send()

    @pl.when(sends_pieces)
    def _():
        for piece in pieces[-2:]:
            piece.wait_send()


def rim_call(field, side, regions):
    return pl.pallas_call(
        functools.partial(rim_kernel, regions),
        out_shape=jax.ShapeDtypeStruct((field.shape[0], side, field.shape[2]), jnp.float32),
        in_specs=[pl.BlockSpec(memory_space=pl.ANY)],
        out_specs=pl.BlockSpec(memory_space=pltpu.VMEM),
        scratch_shapes=[pltpu.SemaphoreType.DMA((4, PIECES + 1))],
        compiler_params=pltpu.CompilerParams(
            vmem_limit_bytes=RIM_VMEM, collective_id=1, has_side_effects=True
        ),
        name="rim",
    )(field)


def on_device(object_field, probes, patterns, offsets, counts):
    side = probes.shape[-1]
    tile = object_field.shape[1]
    waves, regions = lax.axis_size("wave"), lax.axis_size("region")
    paired = waves == 2 and regions & (regions - 1) == 0
    tables = make_tables(side)
    if paired:
        rim = rim_call(object_field, side, regions)
    else:
        rim = from_behind(object_field[:, :side, :], "region", -1)
    grad, prb = patch_call(offsets, counts, object_field, rim, probes, patterns, tables)
    if paired:
        object_out, probe_total = exchange_call(grad, prb, waves, regions)
        return (object_out, probe_total.reshape((1,) + prb.shape))
    arrived = from_behind(grad[:, :, tile:, :], "region", 1)
    probe_total = lax.psum(prb, "region")
    bottom = wave_sum(grad[:, :, side:tile, :])
    top = wave_sum(grad[:, :, :side, :] + arrived)
    return (jnp.concatenate([top, bottom], axis=1), probe_total[None])


def solution(mesh):
    in_specs = (
        P(None, "region", None),
        P("wave", None, None, None),
        P("wave", "region", None, None),
        P("region", None),
        P("region"),
    )
    out_specs = (P(None, "region", "wave"), P("wave", None, None, None))
    return jax.shard_map(
        on_device, mesh=mesh, in_specs=in_specs, out_specs=out_specs, check_vma=False
    )
```
